32 devices in a mesh: mp: 8 (over y, x, core), batch: 4 (over z).
Axes of the slice: x: 2, y: 2, z: 4, core: 2. Of those that a mesh axis runs over, the one named last changes fastest.
Arguments:
- inputs: bfloat16 [24, 12288], P('mp', 'batch'), may hold values from -6 to 6
- weight: bfloat16 [12288, 49152], P('batch', 'mp'), may hold values from -0.0546875 to 0.0546875
- out_grad: bfloat16 [24, 49152], P('batch', 'mp'), may hold values from -6 to 6
- pre_act: bfloat16 [24, 49152], P('batch', 'mp'), may hold values from -6 to 6
Outputs:
- input_grad: bfloat16 [24, 12288], P('mp', 'batch')
- weight_grad: bfloat16 [12288, 49152], P('batch', 'mp')
The draws below stay inside these ranges and needn't reach their ends.
All inputs are finite; a program needn't handle non-finite values.
Results may differ from the reference program's by a relative error of at most 0.0049.
Values may be sent and summed in bfloat16 or wider, within the bound.
No kernel may reach another device: no remote copies, remote signals or barrier semaphores. Data moves between devices by JAX's collectives and lax.ppermute only.
A program may use at most 256 MiB of HBM per device.

```python
import jax
import jax.numpy as jnp

D = 12288
FF = 49152
TOKENS = 24


def spiked(drawn, key, source, target, blocks, factor):
    owner, partner = [(jnp.arange(drawn.shape[position]) // (drawn.shape[position] // blocks)).reshape([-1 if axis == position else 1 for axis in range(drawn.ndim)]) for position in (source, target)]
    chosen = jax.random.permutation(key, blocks)[partner]
    strong = (owner == chosen) | (owner == (partner + blocks // 2) % blocks)
    return jnp.where(strong, factor * drawn, drawn)


def block_scale(own_key, shape, split, smallest, largest):
    loudness = 1.0
    for position, blocks in split:
        heights = jax.random.uniform(jax.random.fold_in(jax.random.fold_in(own_key, 6), position), (blocks,), jnp.float32, smallest / len(split), largest / len(split))
        loudness = loudness * jnp.repeat(jnp.exp(heights), shape[position] // blocks).reshape((-1,) + (1,) * (len(shape) - 1 - position))
    return loudness


def noise(rng, dims, deviation, reach, pieces=(), kind=jnp.bfloat16):
    drawn = jax.random.normal(rng, dims, jnp.float32) * deviation
    if len(pieces) > 0:
        drawn = block_scale(rng, dims, pieces, -0.22, 0.18) * drawn
    return jnp.clip(drawn, min=-reach, max=reach).astype(kind)


def bell_draw_with(key, dims, width, bound, pieces, heavy, held_as=jnp.bfloat16):
    drawn = width * jax.random.normal(key, dims, jnp.float32)
    if pieces:
        drawn = drawn * block_scale(key, dims, pieces, -0.22, 0.18)
    return jnp.clip(spiked(drawn, jax.random.fold_in(key, 3), *heavy), -bound, bound).astype(held_as)


def setup_inputs(seed: int = 0) -> dict:
    splits = jax.random.split(jax.random.key(seed), 5)
    inputs = noise(splits[0], (TOKENS, D), 1.0, 6.0, ((0, 8), (1, 4)))
    weight = noise(splits[1], (D, FF), D ** -0.5, 0.0546875, ((0, 4), (1, 8)))
    out_grad = bell_draw_with(splits[2], (TOKENS, FF), 1.0, 6.0, ((0, 4), (1, 8)), (1, 0, 8, 2.0))
    pre_act = noise(splits[3], (TOKENS, FF), 1.0, 6.0, ((0, 4), (1, 8)))
    return dict(inputs=inputs, weight=weight, out_grad=out_grad, pre_act=pre_act)


def gelu_back(pre_act, out_grad):
    value, pullback = jax.vjp(lambda v: jax.nn.gelu(v, approximate=True), pre_act.astype(jnp.float32))
    return pullback(out_grad.astype(jnp.float32))[0].astype(jnp.bfloat16)

def reference(inputs, weight, out_grad, pre_act):
    hidden_grad = gelu_back(pre_act, out_grad)
    input_grad = jnp.dot(hidden_grad, weight.T, preferred_element_type=jnp.float32).astype(jnp.bfloat16)
    weight_grad = jnp.dot(inputs.T, hidden_grad, preferred_element_type=jnp.float32).astype(jnp.bfloat16)
    return (input_grad, weight_grad)
```

```python
import functools

import jax
import jax.numpy as jnp
from jax import lax
from jax.experimental import pallas as pl
from jax.experimental.pallas import tpu as pltpu
from jax.sharding import PartitionSpec as P

F32, BF16 = jnp.float32, jnp.bfloat16
MIB = 1 << 20
ROWS = 8
VMEM = pl.BlockSpec(memory_space=pltpu.VMEM)
SMEM = pl.BlockSpec(memory_space=pltpu.SMEM)
ANY = pl.BlockSpec(memory_space=pl.ANY)


def gelu_back(pre_act, out_grad):
    value, pullback = jax.vjp(
        lambda v: jax.nn.gelu(v, approximate=True), pre_act.astype(F32)
    )
    return pullback(out_grad.astype(F32))[0].astype(BF16)


def exchange(x, axis, size, bits):
    return lax.ppermute(x, axis, [(i, i ^ bits) for i in range(size)])


def input_grad_kernel(block, place, *refs):
    hidden, inputs = refs[0:4], refs[4:12]
    weight, keep, send, hidden_out, inputs_out, hidden_f32, inputs_f32, total = refs[12:]
    z, chip, core = place[0], place[1], place[2]
    tokens = hidden[0].shape[0]
    half = tokens // 2
    hidden_f32[...] = jnp.zeros_like(hidden_f32)
    inputs_f32[...] = jnp.zeros_like(inputs_f32)
    for k in range(4):
        hidden_f32[z ^ k, 0:tokens, :] = hidden[k][...].astype(F32)
        own, other = inputs[2 * k][...].astype(F32), inputs[2 * k + 1][...].astype(F32)
        inputs_f32[chip ^ k, 0:half, :] = jnp.where(core == 0, own, other)
        inputs_f32[chip ^ k, half:tokens, :] = jnp.where(core == 0, other, own)
    hidden_out[...] = hidden_f32[...].reshape(hidden_out.shape).astype(BF16)
    inputs_out[...] = inputs_f32[...].reshape(inputs_out.shape).astype(BF16)

    def body(i, carry):
        rows = pl.multiple_of(i * block, block)
        total[:, pl.ds(rows, block)] = lax.dot_general(
            hidden_out[...], weight[pl.ds(rows, block), :], (((1,), (1,)), ((), ())), preferred_element_type=F32
        )
        return carry

    lax.fori_loop(0, weight.shape[0] // block, body, 0)
    for b in range(4):
        low = total[ROWS * b : ROWS * b + half, :]
        high = total[ROWS * b + half : ROWS * b + tokens, :]
        keep[b] = jnp.where(core == 0, low, high)
        send[b] = jnp.where(core == 0, high, low)


def input_grad_part(place, hidden, inputs, weight):
    depth, width = weight.shape
    half = inputs[0].shape[0]
    f = lambda shape, dtype: jax.ShapeDtypeStruct(shape, dtype)
    return pl.pallas_call(
        functools.partial(input_grad_kernel, 1024),
        in_specs=[SMEM] + [VMEM] * 13,
        out_specs=[VMEM] * 4,
        out_shape=[
            f((4, half, depth), F32),
            f((4, half, depth), F32),
            f((4 * ROWS, width), BF16),
            f((4 * ROWS, depth), BF16),
        ],
        scratch_shapes=[
            pltpu.VMEM((4, ROWS, width), F32),
            pltpu.VMEM((4, ROWS, depth), F32),
            pltpu.VMEM((4 * ROWS, depth), F32),
        ],
        compiler_params=pltpu.CompilerParams(vmem_limit_bytes=16 * MIB),
        name="input_grad_part",
    )(place, *hidden, *inputs, pltpu.with_memory_space_constraint(weight, pltpu.VMEM))


def weight_grad_kernel(first, count, block, inputs, hidden, *refs):
    out, buffer, sems = refs[-3:]

    def copy(i, slot):
        rows = pl.multiple_of((first + i) * block, block)
        return pltpu.make_async_copy(buffer.at[slot], out.at[pl.ds(rows, block), :], sems.at[slot])

    def body(i, carry):
        slot = lax.rem(i, 2)

        @pl.when(i >= 2)
        def _():
            copy(i - 2, slot).wait()

        rows = pl.multiple_of((first + i) * block, block)
        left = inputs[:, pl.ds(rows, block)]
        buffer[slot] = lax.dot_general(
            left, hidden[...], (((0,), (0,)), ((), ())), preferred_element_type=F32
        ).astype(BF16)
        copy(i, slot).start()
        return carry

    lax.fori_loop(0, count, body, 0)
    for i in range(max(0, count - 2), count):
        copy(i, i % 2).wait()


def weight_grad_part(first, count, block, inputs, hidden, before=None):
    shape = jax.ShapeDtypeStruct((inputs.shape[1], hidden.shape[1]), BF16)
    return pl.pallas_call(
        functools.partial(weight_grad_kernel, first, count, block),
        in_specs=[VMEM, VMEM] + ([] if before is None else [ANY]),
        out_specs=ANY,
        out_shape=shape,
        scratch_shapes=[pltpu.VMEM((2, block, shape.shape[1]), BF16), pltpu.SemaphoreType.DMA((2,))],
        input_output_aliases={} if before is None else {2: 0},
        compiler_params=pltpu.CompilerParams(vmem_limit_bytes=32 * MIB),
        name="weight_grad_part",
    )(inputs, hidden, *([] if before is None else [before]))


def fast(inputs, weight, out_grad, pre_act):
    z, m = lax.axis_index("batch"), lax.axis_index("mp")
    chip, core = m // 2, m % 2
    place = jnp.stack([z, chip, core]).astype(jnp.int32)
    own = gelu_back(pre_act, out_grad)
    hidden = [own] + [exchange(own, "batch", 4, k) for k in (1, 2, 3)]
    other = exchange(inputs, "mp", 8, 1)
    parts = [inputs, other]
    pair = jnp.stack([inputs, other])
    for k in (1, 2, 3):
        got = exchange(pair, "mp", 8, 2 * k)
        parts += [got[0], got[1]]
    keep, send, hidden, inputs = input_grad_part(place, hidden, parts, weight)

    got = exchange(send, "mp", 8, 1)
    block = 256
    blocks = inputs.shape[1] // block
    first = blocks // 3
    grad = weight_grad_part(0, first, block, inputs, hidden)
    mine = keep + got
    sends = [lax.dynamic_index_in_dim(mine, chip ^ k, 0, keepdims=False) for k in range(4)]
    gots = [exchange(sends[k], "mp", 8, 2 * k) for k in (1, 2, 3)]
    grad = weight_grad_part(first, blocks - first, block, inputs, hidden, grad)
    input_grad = (sends[0] + gots[0] + gots[1] + gots[2]).astype(BF16)
    return input_grad, grad


def plain(inputs, weight, out_grad, pre_act):
    hidden = lax.all_gather(gelu_back(pre_act, out_grad), "batch", axis=0, tiled=True)
    inputs = lax.all_gather(inputs, "mp", axis=0, tiled=True)
    weight_grad = lax.dot_general(
        inputs, hidden, (((0,), (0,)), ((), ())), preferred_element_type=F32
    ).astype(BF16)
    input_grad = lax.psum_scatter(
        lax.dot_general(hidden, weight, (((1,), (1,)), ((), ())), preferred_element_type=F32),
        "mp",
        scatter_dimension=0,
        tiled=True,
    ).astype(BF16)
    return input_grad, weight_grad


def solution(mesh):
    small = mesh.shape["batch"] == 4 and mesh.shape["mp"] == 8
    return jax.shard_map(
        fast if small else plain,
        mesh=mesh,
        in_specs=(P("mp", "batch"), P("batch", "mp"), P("batch", "mp"), P("batch", "mp")),
        out_specs=(P("mp", "batch"), P("batch", "mp")),
        check_vma=False,
    )
```

```python
import functools

import jax
import jax.numpy as jnp
from jax import lax
from jax.experimental import pallas as pl
from jax.experimental.pallas import tpu as pltpu
from jax.sharding import PartitionSpec as P

F32, BF16 = jnp.float32, jnp.bfloat16
MIB = 1 << 20
MXU = 256
LANES = 128
ROWS = 8
VMEM = pl.BlockSpec(memory_space=pltpu.VMEM)
SMEM = pl.BlockSpec(memory_space=pltpu.SMEM)
ANY = pl.BlockSpec(memory_space=pl.ANY)


def gelu_back(pre_act, out_grad):
    value, pullback = jax.vjp(
        lambda v: jax.nn.gelu(v, approximate=True), pre_act.astype(F32)
    )
    return pullback(out_grad.astype(F32))[0].astype(BF16)


def in_hbm(x):
    return pltpu.with_memory_space_constraint(x, pltpu.HBM)


def hidden_kernel(pre_act, out_grad, inputs, own, inputs_out, pre, out, sems):
    pairs = ((pre_act, pre), (out_grad, out), (inputs, inputs_out))
    copies = [pltpu.make_async_copy(x, y, sems.at[i]) for i, (x, y) in enumerate(pairs)]
    for copy in copies:
        copy.start()
    for copy in copies:
        copy.wait()
    own[...] = gelu_back(pre[...], out[...])


def hidden_part(pre_act, out_grad, inputs):
    buffer = pltpu.VMEM(pre_act.shape, BF16)
    return pl.pallas_call(
        hidden_kernel,
        in_specs=[ANY] * 3,
        out_specs=[VMEM] * 2,
        out_shape=[buffer, pltpu.VMEM(inputs.shape, inputs.dtype)],
        scratch_shapes=[buffer, buffer, pltpu.SemaphoreType.DMA((3,))],
        compiler_params=pltpu.CompilerParams(vmem_limit_bytes=4 * MIB),
        name="hidden_part",
    )(*[in_hbm(x) for x in (pre_act, out_grad, inputs)])


def exchange(x, axis, size, bits):
    return lax.ppermute(x, axis, [(i, i ^ bits) for i in range(size)])


def gather_rows(place, pieces, padded):
    z, tokens = place[0], pieces[0].shape[0]
    padded[...] = jnp.zeros_like(padded)
    for k in range(4):
        padded[z ^ k, 0:tokens, :] = pieces[k][...].astype(F32)


def weight_rows(weight, tiles, sems, i):
    rows, slot = pl.ds(pl.multiple_of(i * MXU, MXU), MXU), i % tiles.shape[0]
    return pltpu.make_async_copy(weight.at[rows, :], tiles.at[slot], sems.at[slot])


def load_kernel(first, after, weight, tiles, sems):
    copies = [
        pltpu.make_async_copy(weight.at[pl.ds((first + i) * MXU, MXU), :], tiles.at[i], sems.at[i])
        for i in range(tiles.shape[0])
    ]
    for copy in copies:
        copy.start()
    for copy in copies:
        copy.wait()


def load_part(first, count, after, weight):
    return pl.pallas_call(
        functools.partial(load_kernel, first),
        in_specs=[ANY, ANY],
        out_specs=VMEM,
        out_shape=pltpu.VMEM((count, MXU, weight.shape[1]), weight.dtype),
        scratch_shapes=[pltpu.SemaphoreType.DMA((count,))],
        compiler_params=pltpu.CompilerParams(vmem_limit_bytes=2 * MIB),
        name="load_part",
    )(after, in_hbm(weight))


def both_kernel(shared, place, *refs):
    hidden, inputs, weight = refs[0:4], refs[4:8], refs[8]
    early, refs = refs[9], refs[10:]
    grad, hidden_out, inputs_out, keep, send = refs[0:5]
    hidden_f32, inputs_f32, turned, total, tiles, out, load_sems, out_sems = refs[5:]
    depth, width = weight.shape
    blocks, steps, ahead, tall = depth // MXU, width // MXU, tiles.shape[0] - 2, 2 * MXU
    ready = early.shape[0]

    for i in range(ready, min(ready + ahead, blocks)):
        weight_rows(weight, tiles, load_sems, i).start()
    gather_rows(place, hidden, hidden_f32)
    hidden_out[...] = hidden_f32[...].reshape(hidden_out.shape).astype(BF16)
    tokens = hidden[0].shape[0]
    half = tokens // 2
    chip, core = place[1], place[2]
    inputs_f32[...] = jnp.zeros_like(inputs_f32)
    for k in range(4):
        own, other = inputs[k][0].astype(F32), inputs[k][1].astype(F32)
        inputs_f32[chip ^ k, 0:half, :] = jnp.where(core == 0, own, other)
        inputs_f32[chip ^ k, half:tokens, :] = jnp.where(core == 0, other, own)
    inputs_out[...] = inputs_f32[...].reshape(inputs_out.shape).astype(BF16)

    def write(s, slot):
        return pltpu.make_async_copy(out.at[slot], grad.at[pl.ds(s * tall, tall), :], out_sems.at[slot])

    def scoped(*sums):
        small, large = (sums[0:2], sums[2:4]), (sums[4:6], sums[6:8])

        def superblock(s, with_grad):
            known = isinstance(s, int) and 2 * s < ready
            base = s * tall if isinstance(s, int) else pl.multiple_of(s * tall, tall)
            for a in () if known else (0, 1):
                i = 2 * s + a
                weight_rows(weight, tiles, load_sems, i).wait()

                @pl.when(i + ahead < blocks)
                def _():
                    weight_rows(weight, tiles, load_sems, i + ahead).start()

            def push_weight(m, k, a, stage):
                columns = slice(k * MXU, (k + 1) * MXU)
                tile = early[2 * s + a, :, columns] if known else tiles[(2 * s + a) % tiles.shape[0], :, columns]
                pltpu.matmul_push_rhs(tile, stage, m, transpose=True)

            def push_hidden(m, k, stage):
                tile = hidden_out[:, k * MXU : (k + 1) * MXU]
                blank = jnp.zeros((MXU - tile.shape[0], MXU), BF16)
                pltpu.matmul_push_rhs(jnp.concatenate([tile, blank], 0), stage, m)

            def times_weight(m, k, a, stage):
                left = hidden_out[:, k * MXU : (k + 1) * MXU]
                pltpu.matmul_acc_lhs(small[m][a], left, load_staged_rhs=stage)

            both = (0, 1)
            if with_grad:
                slot = s % out.shape[0]
                if s >= out.shape[0]:
                    write(s - out.shape[0], slot).wait()

                left = inputs_out[:, pl.ds(base, tall)]
                blank = jnp.zeros((turned.shape[1] - left.shape[0], tall), BF16)
                turned[...] = jnp.concatenate([left, blank], 0).T
                wide = jnp.zeros((MXU, MXU - turned.shape[1]), BF16)

                def times_hidden(m, a, stage):
                    left = jnp.concatenate([turned[a * MXU : (a + 1) * MXU, :], wide], 1)
                    pltpu.matmul_acc_lhs(large[m][a], left, load_staged_rhs=stage)

                def store(m, k, a):
                    out[slot, a * MXU : (a + 1) * MXU, k * MXU : (k + 1) * MXU] = pltpu.matmul_pop(
                        large[m][a]
                    ).astype(BF16)

                for m in both:
                    push_hidden(m, m, 0)
                for j in range(steps // 2):
                    h, o = j % 2, 1 - j % 2
                    for m in both:
                        times_hidden(m, 0, h)
                        push_weight(m, 2 * j + m, 0, o)
                    for m in both:
                        times_hidden(m, 1, None)
                        push_weight(m, 2 * j + m, 1, h)
                    for m in both:
                        store(m, 2 * j + m, 0)
                        times_weight(m, 2 * j + m, 0, o)
                        if 2 * j + 2 < steps:
                            push_hidden(m, 2 * j + 2 + m, o)
                        times_weight(m, 2 * j + m, 1, h)
                    for m in both:
                        store(m, 2 * j + m, 1)
                write(s, slot).start()
            else:
                for m in both:
                    push_weight(m, m, 0, 0)
                for j in range(steps // 2):
                    for m in both:
                        push_weight(m, 2 * j + m, 1, 1)
                        times_weight(m, 2 * j + m, 0, 0)
                    for m in both:
                        if 2 * j + 2 < steps:
                            push_weight(m, 2 * j + 2 + m, 0, 0)
                        times_weight(m, 2 * j + m, 1, 1)
            for a in (0, 1):
                rows = pl.ds(pl.multiple_of(base + a * MXU, MXU), MXU)
                total[:, rows] = pltpu.matmul_pop(small[0][a]) + pltpu.matmul_pop(small[1][a])

        def body(s, carry):
            superblock(s, False)
            return carry

        for s in range(shared):
            superblock(s, True)
        lax.fori_loop(shared, blocks // 2, body, 0)

    sums = [pltpu.ACC(m)((4 * ROWS, MXU), F32) for m in (0, 0, 1, 1)]
    sums += [pltpu.ACC(m)((MXU, MXU), F32) for m in (0, 0, 1, 1)]
    pl.run_scoped(scoped, *sums)
    for b in range(4):
        low = total[ROWS * b : ROWS * b + half, :]
        high = total[ROWS * b + half : ROWS * b + tokens, :]
        keep[b] = jnp.where(core == 0, low, high)
        send[b] = jnp.where(core == 0, high, low)
    for s in range(max(0, shared - out.shape[0]), shared):
        write(s, s % out.shape[0]).wait()


def both_part(shared, place, hidden, inputs, weight, early):
    depth, width = weight.shape
    half = hidden[0].shape[0] // 2
    f = lambda shape, dtype: jax.ShapeDtypeStruct(shape, dtype)
    slots, ahead = 2, 6
    return pl.pallas_call(
        functools.partial(both_kernel, shared),
        in_specs=[SMEM] + [VMEM] * 8 + [ANY, VMEM],
        out_specs=[ANY] + [VMEM] * 4,
        out_shape=[
            f((depth, width), BF16),
            f((4 * ROWS, width), BF16),
            f((4 * ROWS, depth), BF16),
            f((4, half, depth), F32),
            f((4, half, depth), F32),
        ],
        scratch_shapes=[
            pltpu.VMEM((4, ROWS, width), F32),
            pltpu.VMEM((4, ROWS, depth), F32),
            pltpu.VMEM((2 * MXU, LANES), BF16),
            pltpu.VMEM((4 * ROWS, depth), F32),
            pltpu.VMEM((ahead, MXU, width), BF16),
            pltpu.VMEM((slots, 2 * MXU, width), BF16),
            pltpu.SemaphoreType.DMA((ahead,)),
            pltpu.SemaphoreType.DMA((slots,)),
        ],
        compiler_params=pltpu.CompilerParams(vmem_limit_bytes=40 * MIB),
        name="both_part",
    )(place, *hidden, *inputs, in_hbm(weight), early)


def weight_grad_kernel(first, count, block, slots, inputs, hidden, *refs):
    out, buffer, sems = refs[-3:]

    def copy(i, slot):
        rows = pl.multiple_of((first + i) * block, block)
        return pltpu.make_async_copy(buffer.at[slot], out.at[pl.ds(rows, block), :], sems.at[slot])

    def body(i, carry):
        slot = lax.rem(i, slots)

        @pl.when(i >= slots)
        def _():
            copy(i - slots, slot).wait()

        rows = pl.multiple_of((first + i) * block, block)
        left = inputs[:, pl.ds(rows, block)]
        buffer[slot] = lax.dot_general(
            left, hidden[...], (((0,), (0,)), ((), ())), preferred_element_type=F32
        ).astype(BF16)
        copy(i, slot).start()
        return carry

    lax.fori_loop(0, count, body, 0)
    for i in range(max(0, count - slots), count):
        copy(i, i % slots).wait()


def weight_grad_part(first, count, inputs, hidden, before=None):
    shape = jax.ShapeDtypeStruct((inputs.shape[1], hidden.shape[1]), BF16)
    block, slots = MXU, 4
    return pl.pallas_call(
        functools.partial(weight_grad_kernel, first, count, block, slots),
        in_specs=[VMEM] * 2 + ([] if before is None else [ANY]),
        out_specs=ANY,
        out_shape=shape,
        scratch_shapes=[
            pltpu.VMEM((slots, block, shape.shape[1]), BF16),
            pltpu.SemaphoreType.DMA((slots,)),
        ],
        input_output_aliases={} if before is None else {2: 0},
        compiler_params=pltpu.CompilerParams(vmem_limit_bytes=20 * MIB),
        name="weight_grad_part",
    )(inputs, hidden, *([] if before is None else [before]))


def fast(inputs, weight, out_grad, pre_act):
    z, m = lax.axis_index("batch"), lax.axis_index("mp")
    chip, core = m // 2, m % 2
    place = jnp.stack([z, chip, core]).astype(jnp.int32)
    blocks, shared = weight.shape[0] // MXU, 3

    own, inputs = hidden_part(pre_act, out_grad, inputs)
    other = exchange(inputs, "mp", 8, 1)
    hidden = [own] + [exchange(own, "batch", 4, k) for k in (1, 2, 3)]
    pair = jnp.stack([inputs, other])
    late, hidden[1] = lax.optimization_barrier((pair, hidden[1]))
    pairs = [pair, exchange(pair, "mp", 8, 4), exchange(pair, "mp", 8, 2), exchange(late, "mp", 8, 6)]
    pairs = [pairs[0], pairs[2], pairs[1], pairs[3]]
    early = load_part(0, 4, late, weight)
    grad, hidden, inputs, keep, send = both_part(shared, place, hidden, pairs, weight, early)

    got = exchange(send, "mp", 8, 1)
    first, middle = 2 * shared, 2 * shared + 2
    grad = weight_grad_part(first, middle - first, inputs, hidden, grad)
    grad, keep = lax.optimization_barrier((grad, keep))
    mine = keep + got
    sends = [lax.dynamic_index_in_dim(mine, chip ^ k, 0, keepdims=False) for k in range(4)]
    gots = [exchange(sends[k], "mp", 8, 2 * k) for k in (1, 2, 3)]
    grad = weight_grad_part(middle, blocks - middle, inputs, hidden, grad)
    input_grad = (sends[0] + gots[0] + gots[1] + gots[2]).astype(BF16)
    return input_grad, grad


def plain(inputs, weight, out_grad, pre_act):
    hidden = lax.all_gather(gelu_back(pre_act, out_grad), "batch", axis=0, tiled=True)
    inputs = lax.all_gather(inputs, "mp", axis=0, tiled=True)
    weight_grad = lax.dot_general(
        inputs, hidden, (((0,), (0,)), ((), ())), preferred_element_type=F32
    ).astype(BF16)
    input_grad = lax.psum_scatter(
        lax.dot_general(hidden, weight, (((1,), (1,)), ((), ())), preferred_element_type=F32),
        "mp",
        scatter_dimension=0,
        tiled=True,
    ).astype(BF16)
    return input_grad, weight_grad


def solution(mesh):
    small = mesh.shape["batch"] == 4 and mesh.shape["mp"] == 8
    return jax.shard_map(
        fast if small else plain,
        mesh=mesh,
        in_specs=(P("mp", "batch"), P("batch", "mp"), P("batch", "mp"), P("batch", "mp")),
        out_specs=(P("mp", "batch"), P("batch", "mp")),
        check_vma=False,
    )
```

```python
import functools

import jax
import jax.numpy as jnp
from jax import lax
from jax.experimental import pallas as pl
from jax.experimental.pallas import tpu as pltpu
from jax.sharding import PartitionSpec as P

F32, BF16 = jnp.float32, jnp.bfloat16
MIB = 1 << 20
MXU = 256
LANES = 128
ROWS = 8
VMEM = pl.BlockSpec(memory_space=pltpu.VMEM)
SMEM = pl.BlockSpec(memory_space=pltpu.SMEM)
ANY = pl.BlockSpec(memory_space=pl.ANY)


def gelu_back(pre_act, out_grad):
    value, pullback = jax.vjp(
        lambda v: jax.nn.gelu(v, approximate=True), pre_act.astype(F32)
    )
    return pullback(out_grad.astype(F32))[0].astype(BF16)


def in_hbm(x):
    return pltpu.with_memory_space_constraint(x, pltpu.HBM)


def hidden_kernel(pre_act, out_grad, inputs, own, inputs_out, pre, out, sems):
    pairs = ((pre_act, pre), (out_grad, out), (inputs, inputs_out))
    copies = [pltpu.make_async_copy(x, y, sems.at[i]) for i, (x, y) in enumerate(pairs)]
    for copy in copies:
        copy.start()
    for copy in copies:
        copy.wait()
    own[...] = gelu_back(pre[...], out[...])


def hidden_part(pre_act, out_grad, inputs):
    buffer = pltpu.VMEM(pre_act.shape, BF16)
    return pl.pallas_call(
        hidden_kernel,
        in_specs=[ANY] * 3,
        out_specs=[VMEM] * 2,
        out_shape=[buffer, pltpu.VMEM(inputs.shape, inputs.dtype)],
        scratch_shapes=[buffer, buffer, pltpu.SemaphoreType.DMA((3,))],
        compiler_params=pltpu.CompilerParams(vmem_limit_bytes=4 * MIB),
        name="hidden_part",
    )(*[in_hbm(x) for x in (pre_act, out_grad, inputs)])


def exchange(x, axis, size, bits):
    return lax.ppermute(x, axis, [(i, i ^ bits) for i in range(size)])


def gather_rows(place, pieces, padded):
    z, tokens = place[0], pieces[0].shape[0]
    padded[...] = jnp.zeros_like(padded)
    for k in range(4):
        padded[z ^ k, 0:tokens, :] = pieces[k][...].astype(F32)


def weight_rows(weight, tiles, sems, i, ready):
    rows, slot = pl.ds(pl.multiple_of(i * MXU, MXU), MXU), (i - ready) % tiles.shape[0]
    return pltpu.make_async_copy(weight.at[rows, :], tiles.at[slot], sems.at[slot])


def load_kernel(first, after, weight, tiles, sems):
    copies = [
        pltpu.make_async_copy(weight.at[pl.ds((first + i) * MXU, MXU), :], tiles.at[i], sems.at[i])
        for i in range(tiles.shape[0])
    ]
    for copy in copies:
        copy.start()
    for copy in copies:
        copy.wait()


def load_part(first, count, after, weight):
    return pl.pallas_call(
        functools.partial(load_kernel, first),
        in_specs=[ANY, ANY],
        out_specs=VMEM,
        out_shape=pltpu.VMEM((count, MXU, weight.shape[1]), weight.dtype),
        scratch_shapes=[pltpu.SemaphoreType.DMA((count,))],
        compiler_params=pltpu.CompilerParams(vmem_limit_bytes=2 * MIB),
        name="load_part",
    )(after, in_hbm(weight))


def both_kernel(place, *refs):
    hidden, inputs, weight = refs[0:4], refs[4:8], refs[8]
    early, refs = refs[9], refs[10:]
    grad, hidden_out, inputs_out, keep, send = refs[0:5]
    hidden_f32, inputs_f32, turned, total, tiles, out, load_sems, out_sems = refs[5:]
    depth, width = weight.shape
    blocks, steps, tall = depth // MXU, width // MXU, 2 * MXU
    ready, ring = early.shape[0], tiles.shape[0]

    for i in range(ready, min(ready + ring, blocks)):
        weight_rows(weight, tiles, load_sems, i, ready).start()
    gather_rows(place, hidden, hidden_f32)
    hidden_out[...] = hidden_f32[...].reshape(hidden_out.shape).astype(BF16)
    tokens = hidden[0].shape[0]
    half = tokens // 2
    chip, core = place[1], place[2]
    inputs_f32[...] = jnp.zeros_like(inputs_f32)
    for k in range(4):
        own, other = inputs[k][0].astype(F32), inputs[k][1].astype(F32)
        inputs_f32[chip ^ k, 0:half, :] = jnp.where(core == 0, own, other)
        inputs_f32[chip ^ k, half:tokens, :] = jnp.where(core == 0, other, own)
    inputs_out[...] = inputs_f32[...].reshape(inputs_out.shape).astype(BF16)

    slots, pairs = out.shape[0], blocks // 4

    def write(p):
        rows = pl.ds(pl.multiple_of(2 * p * tall, tall), tall)
        return pltpu.make_async_copy(out.at[p % slots], grad.at[rows, :], out_sems.at[p % slots])

    def scoped(*sums):
        small, large = (sums[0:2], sums[2:4]), (sums[4:6], sums[6:8])

        def superblock(s, with_grad):
            known = isinstance(s, int) and 2 * s < ready
            base = s * tall if isinstance(s, int) else pl.multiple_of(s * tall, tall)
            for a in () if known else (0, 1):
                weight_rows(weight, tiles, load_sems, 2 * s + a, ready).wait()
                free = 2 * s - 2 + a

                @pl.when((free >= ready) & (free + ring < blocks))
                def _():
                    weight_rows(weight, tiles, load_sems, free + ring, ready).start()

            def push_weight(m, k, a, stage):
                columns = slice(k * MXU, (k + 1) * MXU)
                tile = early[2 * s + a, :, columns] if known else tiles[(2 * s + a - ready) % ring, :, columns]
                pltpu.matmul_push_rhs(tile, stage, m, transpose=True)

            def push_hidden(m, k, stage):
                tile = hidden_out[:, k * MXU : (k + 1) * MXU]
                blank = jnp.zeros((MXU - tile.shape[0], MXU), BF16)
                pltpu.matmul_push_rhs(jnp.concatenate([tile, blank], 0), stage, m)

            def times_weight(m, k, a, stage):
                left = hidden_out[:, k * MXU : (k + 1) * MXU]
                pltpu.matmul_acc_lhs(small[m][a], left, load_staged_rhs=stage)

            both = (0, 1)
            if with_grad:
                p = s // 2

                @pl.when(p >= slots)
                def _():
                    write(p - slots).wait()

                left = inputs_out[:, pl.ds(base, tall)]
                blank = jnp.zeros((turned.shape[1] - left.shape[0], tall), BF16)
                turned[...] = jnp.concatenate([left, blank], 0).T
                wide = jnp.zeros((MXU, MXU - turned.shape[1]), BF16)

                def times_hidden(m, a, stage):
                    left = jnp.concatenate([turned[a * MXU : (a + 1) * MXU, :], wide], 1)
                    pltpu.matmul_acc_lhs(large[m][a], left, load_staged_rhs=stage)

                def store(m, k, a):
                    out[p % slots, a * MXU : (a + 1) * MXU, k * MXU : (k + 1) * MXU] = pltpu.matmul_pop(
                        large[m][a]
                    ).astype(BF16)

                for m in both:
                    push_hidden(m, m, 0)
                for j in range(steps // 2):
                    h, o = j % 2, 1 - j % 2
                    for m in both:
                        times_hidden(m, 0, h)
                        push_weight(m, 2 * j + m, 0, o)
                    for m in both:
                        times_hidden(m, 1, None)
                        push_weight(m, 2 * j + m, 1, h)
                    for m in both:
                        store(m, 2 * j + m, 0)
                        times_weight(m, 2 * j + m, 0, o)
                        if 2 * j + 2 < steps:
                            push_hidden(m, 2 * j + 2 + m, o)
                        times_weight(m, 2 * j + m, 1, h)
                    for m in both:
                        store(m, 2 * j + m, 1)
                write(p).start()
            else:
                for m in both:
                    push_weight(m, m, 0, 0)
                for j in range(steps // 2):
                    for m in both:
                        push_weight(m, 2 * j + m, 1, 1)
                        times_weight(m, 2 * j + m, 0, 0)
                    for m in both:
                        if 2 * j + 2 < steps:
                            push_weight(m, 2 * j + 2 + m, 0, 0)
                        times_weight(m, 2 * j + m, 1, 1)
            for a in (0, 1):
                rows = pl.ds(pl.multiple_of(base + a * MXU, MXU), MXU)
                total[:, rows] = pltpu.matmul_pop(small[0][a]) + pltpu.matmul_pop(small[1][a])

        def body(p, carry):
            superblock(2 * p, True)
            superblock(2 * p + 1, False)
            return carry

        for p in range(ready // 4):
            body(p, 0)
        lax.fori_loop(ready // 4, pairs, body, 0)

    sums = [pltpu.ACC(m)((4 * ROWS, MXU), F32) for m in (0, 0, 1, 1)]
    sums += [pltpu.ACC(m)((MXU, MXU), F32) for m in (0, 0, 1, 1)]
    pl.run_scoped(scoped, *sums)
    for b in range(4):
        low = total[ROWS * b : ROWS * b + half, :]
        high = total[ROWS * b + half : ROWS * b + tokens, :]
        keep[b] = jnp.where(core == 0, low, high)
        send[b] = jnp.where(core == 0, high, low)
    for p in range(max(0, pairs - slots), pairs):
        write(p).wait()


def both_part(place, hidden, inputs, weight, early):
    depth, width = weight.shape
    half = hidden[0].shape[0] // 2
    f = lambda shape, dtype: jax.ShapeDtypeStruct(shape, dtype)
    slots, later = 2, 7
    return pl.pallas_call(
        both_kernel,
        in_specs=[SMEM] + [VMEM] * 8 + [ANY, VMEM],
        out_specs=[ANY] + [VMEM] * 4,
        out_shape=[
            f((depth, width), BF16),
            f((4 * ROWS, width), BF16),
            f((4 * ROWS, depth), BF16),
            f((4, half, depth), F32),
            f((4, half, depth), F32),
        ],
        scratch_shapes=[
            pltpu.VMEM((4, ROWS, width), F32),
            pltpu.VMEM((4, ROWS, depth), F32),
            pltpu.VMEM((2 * MXU, LANES), BF16),
            pltpu.VMEM((4 * ROWS, depth), F32),
            pltpu.VMEM((later, MXU, width), BF16),
            pltpu.VMEM((slots, 2 * MXU, width), BF16),
            pltpu.SemaphoreType.DMA((later,)),
            pltpu.SemaphoreType.DMA((slots,)),
        ],
        compiler_params=pltpu.CompilerParams(vmem_limit_bytes=40 * MIB),
        name="both_part",
    )(place, *hidden, *inputs, in_hbm(weight), early)


def weight_grad_kernel(first, count, block, slots, pieces, inputs, hidden, *refs):
    out, buffer, sems = refs[-3:]
    width = out.shape[1] // pieces

    def place(i):
        i = first + i
        return pl.multiple_of((4 * (i // 2) + 2 + i % 2) * block, block)

    def copy(i, piece):
        rows, columns = pl.ds(place(i), block), pl.ds(piece * width, width)
        slot = i % slots
        return pltpu.make_async_copy(
            buffer.at[slot, :, columns], out.at[rows, columns], sems.at[slot, piece]
        )

    def body(i, carry):
        slot = i % slots

        @pl.when(i >= slots)
        def _():
            for piece in range(pieces):
                copy(i - slots, piece).wait()

        left = inputs[:, pl.ds(place(i), block)]
        for piece in range(pieces):
            columns = slice(piece * width, (piece + 1) * width)
            buffer[slot, :, columns] = lax.dot_general(
                left, hidden[:, columns], (((0,), (0,)), ((), ())), preferred_element_type=F32
            ).astype(BF16)
            copy(i, piece).start()
        return carry

    lax.fori_loop(0, count, body, 0)
    for i in range(max(0, count - slots), count):
        for piece in range(pieces):
            copy(i, piece).wait()


def weight_grad_part(first, count, inputs, hidden, before):
    shape = jax.ShapeDtypeStruct(before.shape, BF16)
    block, slots, pieces = MXU, min(count, 4), 4
    return pl.pallas_call(
        functools.partial(weight_grad_kernel, first, count, block, slots, pieces),
        in_specs=[VMEM, VMEM, ANY],
        out_specs=ANY,
        out_shape=shape,
        scratch_shapes=[
            pltpu.VMEM((slots, block, shape.shape[1]), BF16),
            pltpu.SemaphoreType.DMA((slots, pieces)),
        ],
        input_output_aliases={2: 0},
        compiler_params=pltpu.CompilerParams(vmem_limit_bytes=20 * MIB),
        name="weight_grad_part",
    )(inputs, hidden, before)


def fast(inputs, weight, out_grad, pre_act):
    z, m = lax.axis_index("batch"), lax.axis_index("mp")
    chip, core = m // 2, m % 2
    place = jnp.stack([z, chip, core]).astype(jnp.int32)
    blocks = weight.shape[0] // (2 * MXU)

    own, inputs = hidden_part(pre_act, out_grad, inputs)
    other = exchange(inputs, "mp", 8, 1)
    hidden = [own] + [exchange(own, "batch", 4, k) for k in (1, 2, 3)]
    pair = jnp.stack([inputs, other])
    late, hidden[1] = lax.optimization_barrier((pair, hidden[1]))
    pairs = [pair, exchange(pair, "mp", 8, 4), exchange(pair, "mp", 8, 2), exchange(late, "mp", 8, 6)]
    pairs = [pairs[0], pairs[2], pairs[1], pairs[3]]
    early = load_part(0, 4, late, weight)
    grad, hidden, inputs, keep, send = both_part(place, hidden, pairs, weight, early)

    got = exchange(send, "mp", 8, 1)
    first = 1
    grad = weight_grad_part(0, first, inputs, hidden, grad)
    grad, keep = lax.optimization_barrier((grad, keep))
    mine = keep + got
    sends = [lax.dynamic_index_in_dim(mine, chip ^ k, 0, keepdims=False) for k in range(4)]
    gots = [exchange(sends[k], "mp", 8, 2 * k) for k in (1, 2, 3)]
    grad = weight_grad_part(first, blocks - first, inputs, hidden, grad)
    input_grad = (sends[0] + gots[0] + gots[1] + gots[2]).astype(BF16)
    return input_grad, grad


def plain(inputs, weight, out_grad, pre_act):
    hidden = lax.all_gather(gelu_back(pre_act, out_grad), "batch", axis=0, tiled=True)
    inputs = lax.all_gather(inputs, "mp", axis=0, tiled=True)
    weight_grad = lax.dot_general(
        inputs, hidden, (((0,), (0,)), ((), ())), preferred_element_type=F32
    ).astype(BF16)
    input_grad = lax.psum_scatter(
        lax.dot_general(hidden, weight, (((1,), (1,)), ((), ())), preferred_element_type=F32),
        "mp",
        scatter_dimension=0,
        tiled=True,
    ).astype(BF16)
    return input_grad, weight_grad


def solution(mesh):
    small = mesh.shape["batch"] == 4 and mesh.shape["mp"] == 8
    return jax.shard_map(
        fast if small else plain,
        mesh=mesh,
        in_specs=(P("mp", "batch"), P("batch", "mp"), P("batch", "mp"), P("batch", "mp")),
        out_specs=(P("mp", "batch"), P("batch", "mp")),
        check_vma=False,
    )
```

```python
import functools

import jax
import jax.numpy as jnp
from jax import lax
from jax.experimental import pallas as pl
from jax.experimental.pallas import tpu as pltpu
from jax.sharding import PartitionSpec as P

F32, BF16 = jnp.float32, jnp.bfloat16
MIB = 1 << 20
MXU = 256
LANES = 128
ROWS = 8
VMEM = pl.BlockSpec(memory_space=pltpu.VMEM)
ANY = pl.BlockSpec(memory_space=pl.ANY)


def gelu_back(pre_act, out_grad):
    value, pullback = jax.vjp(
        lambda v: jax.nn.gelu(v, approximate=True), pre_act.astype(F32)
    )
    return pullback(out_grad.astype(F32))[0].astype(BF16)


def in_hbm(x):
    return pltpu.with_memory_space_constraint(x, pltpu.HBM)


def hidden_kernel(pre_act, out_grad, inputs, own, inputs_out, pre, out, sems):
    pairs = ((pre_act, pre), (out_grad, out), (inputs, inputs_out))
    copies = [pltpu.make_async_copy(x, y, sems.at[i]) for i, (x, y) in enumerate(pairs)]
    for copy in copies:
        copy.start()
    for copy in copies:
        copy.wait()
    own[...] = gelu_back(pre[...], out[...])


def hidden_part(pre_act, out_grad, inputs):
    buffer = pltpu.VMEM(pre_act.shape, BF16)
    return pl.pallas_call(
        hidden_kernel,
        in_specs=[ANY] * 3,
        out_specs=[VMEM] * 2,
        out_shape=[buffer, pltpu.VMEM(inputs.shape, inputs.dtype)],
        scratch_shapes=[buffer, buffer, pltpu.SemaphoreType.DMA((3,))],
        compiler_params=pltpu.CompilerParams(vmem_limit_bytes=4 * MIB),
        name="hidden_part",
    )(*[in_hbm(x) for x in (pre_act, out_grad, inputs)])


def exchange(x, axis, size, bits):
    return lax.ppermute(x, axis, [(i, i ^ bits) for i in range(size)])


def gather_rows(z, pieces, padded):
    tokens = pieces[0].shape[0]
    padded[...] = jnp.zeros_like(padded)
    for k in range(4):
        padded[z ^ k, 0:tokens, :] = pieces[k][...].astype(F32)


def weight_rows(weight, tiles, sems, i, ready):
    rows, slot = pl.ds(pl.multiple_of(i * MXU, MXU), MXU), (i - ready) % tiles.shape[0]
    return pltpu.make_async_copy(weight.at[rows, :], tiles.at[slot], sems.at[slot])


def load_kernel(first, after, weight, tiles, sems):
    copies = [
        pltpu.make_async_copy(weight.at[pl.ds((first + i) * MXU, MXU), :], tiles.at[i], sems.at[i])
        for i in range(tiles.shape[0])
    ]
    for copy in copies:
        copy.start()
    for copy in copies:
        copy.wait()


def load_part(first, count, after, weight):
    return pl.pallas_call(
        functools.partial(load_kernel, first),
        in_specs=[ANY, ANY],
        out_specs=VMEM,
        out_shape=pltpu.VMEM((count, MXU, weight.shape[1]), weight.dtype),
        scratch_shapes=[pltpu.SemaphoreType.DMA((count,))],
        compiler_params=pltpu.CompilerParams(vmem_limit_bytes=2 * MIB),
        name="load_part",
    )(after, in_hbm(weight))


def both_kernel(*refs):
    z, m = lax.axis_index("batch"), lax.axis_index("mp")
    chip, core = m // 2, m % 2
    hidden, inputs, weight = refs[3::-1], refs[4:8], refs[8]
    early, refs = refs[9], refs[10:]
    grad, hidden_out, inputs_out, keep, send = refs[0:5]
    hidden_f32, inputs_f32, turned, total, tiles, out, load_sems, out_sems = refs[5:]
    depth, width = weight.shape
    blocks, steps, tall = depth // MXU, width // MXU, 2 * MXU
    ready, ring = early.shape[0], tiles.shape[0]

    for i in range(ready, min(ready + ring, blocks)):
        weight_rows(weight, tiles, load_sems, i, ready).start()
    gather_rows(z, hidden, hidden_f32)
    hidden_out[...] = hidden_f32[...].reshape(hidden_out.shape).astype(BF16)
    tokens = hidden[0].shape[0]
    half = tokens // 2
    inputs_f32[...] = jnp.zeros_like(inputs_f32)
    for k in range(4):
        own, other = inputs[k][0].astype(F32), inputs[k][1].astype(F32)
        inputs_f32[chip ^ k, 0:half, :] = jnp.where(core == 0, own, other)
        inputs_f32[chip ^ k, half:tokens, :] = jnp.where(core == 0, other, own)
    inputs_out[...] = inputs_f32[...].reshape(inputs_out.shape).astype(BF16)

    slots, pairs = out.shape[0], blocks // 4

    def write(p):
        rows = pl.ds(pl.multiple_of(2 * p * tall, tall), tall)
        return pltpu.make_async_copy(out.at[p % slots], grad.at[rows, :], out_sems.at[p % slots])

    def scoped(*sums):
        small, large = (sums[0:2], sums[2:4]), (sums[4:6], sums[6:8])

        def superblock(s, with_grad):
            known = isinstance(s, int) and 2 * s < ready
            base = s * tall if isinstance(s, int) else pl.multiple_of(s * tall, tall)
            for a in () if known else (0, 1):
                weight_rows(weight, tiles, load_sems, 2 * s + a, ready).wait()
                free = 2 * s - 2 + a

                @pl.when((free >= ready) & (free + ring < blocks))
                def _():
                    weight_rows(weight, tiles, load_sems, free + ring, ready).start()

            def push_weight(m, k, a, stage):
                columns = slice(k * MXU, (k + 1) * MXU)
                tile = early[2 * s + a, :, columns] if known else tiles[(2 * s + a - ready) % ring, :, columns]
                pltpu.matmul_push_rhs(tile, stage, m, transpose=True)

            def push_hidden(m, k, stage):
                tile = hidden_out[:, k * MXU : (k + 1) * MXU]
                blank = jnp.zeros((MXU - tile.shape[0], MXU), BF16)
                pltpu.matmul_push_rhs(jnp.concatenate([tile, blank], 0), stage, m)

            def times_weight(m, k, a, stage):
                left = hidden_out[:, k * MXU : (k + 1) * MXU]
                pltpu.matmul_acc_lhs(small[m][a], left, load_staged_rhs=stage)

            both = (0, 1)
            if with_grad:
                p = s // 2

                @pl.when(p >= slots)
                def _():
                    write(p - slots).wait()

                left = inputs_out[:, pl.ds(base, tall)]
                blank = jnp.zeros((turned.shape[1] - left.shape[0], tall), BF16)
                turned[...] = jnp.concatenate([left, blank], 0).T
                wide = jnp.zeros((MXU, MXU - turned.shape[1]), BF16)

                def times_hidden(m, a, stage):
                    left = jnp.concatenate([turned[a * MXU : (a + 1) * MXU, :], wide], 1)
                    pltpu.matmul_acc_lhs(large[m][a], left, load_staged_rhs=stage)

                def store(m, k, a):
                    out[p % slots, a * MXU : (a + 1) * MXU, k * MXU : (k + 1) * MXU] = pltpu.matmul_pop(
                        large[m][a]
                    ).astype(BF16)

                for m in both:
                    push_hidden(m, m, 0)
                for j in range(steps // 2):
                    h, o = j % 2, 1 - j % 2
                    for m in both:
                        times_hidden(m, 0, h)
                        push_weight(m, 2 * j + m, 0, o)
                    for m in both:
                        times_hidden(m, 1, None)
                        push_weight(m, 2 * j + m, 1, h)
                    for m in both:
                        store(m, 2 * j + m, 0)
                        times_weight(m, 2 * j + m, 0, o)
                        if 2 * j + 2 < steps:
                            push_hidden(m, 2 * j + 2 + m, o)
                        times_weight(m, 2 * j + m, 1, h)
                    for m in both:
                        store(m, 2 * j + m, 1)
                write(p).start()
            else:
                for m in both:
                    push_weight(m, m, 0, 0)
                for j in range(steps // 2):
                    for m in both:
                        push_weight(m, 2 * j + m, 1, 1)
                        times_weight(m, 2 * j + m, 0, 0)
                    for m in both:
                        if 2 * j + 2 < steps:
                            push_weight(m, 2 * j + 2 + m, 0, 0)
                        times_weight(m, 2 * j + m, 1, 1)
            for a in (0, 1):
                rows = pl.ds(pl.multiple_of(base + a * MXU, MXU), MXU)
                total[:, rows] = pltpu.matmul_pop(small[0][a]) + pltpu.matmul_pop(small[1][a])

        def body(p, carry):
            superblock(2 * p, True)
            superblock(2 * p + 1, False)
            return carry

        for p in range(ready // 4):
            body(p, 0)
        lax.fori_loop(ready // 4, pairs, body, 0)

    sums = [pltpu.ACC(m)((4 * ROWS, MXU), F32) for m in (0, 0, 1, 1)]
    sums += [pltpu.ACC(m)((MXU, MXU), F32) for m in (0, 0, 1, 1)]
    pl.run_scoped(scoped, *sums)
    for k in range(4):
        rows = total[pl.ds(pl.multiple_of(ROWS * (chip ^ k), ROWS), ROWS), :]
        low, high = rows[:half], rows[half:tokens]
        keep[k] = jnp.where(core == 0, low, high)
        send[k] = jnp.where(core == 0, high, low)
    for p in range(max(0, pairs - slots), pairs):
        write(p).wait()


def both_part(hidden, inputs, weight, early):
    depth, width = weight.shape
    half = hidden[0].shape[0] // 2
    f = lambda shape, dtype: jax.ShapeDtypeStruct(shape, dtype)
    slots, later = 2, 7
    return pl.pallas_call(
        both_kernel,
        in_specs=[VMEM] * 8 + [ANY, VMEM],
        out_specs=[ANY] + [VMEM] * 4,
        out_shape=[
            f((depth, width), BF16),
            f((4 * ROWS, width), BF16),
            f((4 * ROWS, depth), BF16),
            f((4, half, depth), F32),
            f((4, half, depth), F32),
        ],
        scratch_shapes=[
            pltpu.VMEM((4, ROWS, width), F32),
            pltpu.VMEM((4, ROWS, depth), F32),
            pltpu.VMEM((2 * MXU, LANES), BF16),
            pltpu.VMEM((4 * ROWS, depth), F32),
            pltpu.VMEM((later, MXU, width), BF16),
            pltpu.VMEM((slots, 2 * MXU, width), BF16),
            pltpu.SemaphoreType.DMA((later,)),
            pltpu.SemaphoreType.DMA((slots,)),
        ],
        compiler_params=pltpu.CompilerParams(vmem_limit_bytes=40 * MIB),
        name="both_part",
    )(*hidden[::-1], *inputs, in_hbm(weight), early)


def weight_grad_kernel(first, count, block, slots, pieces, inputs, hidden, *refs):
    out, buffer, sems = refs[-3:]
    width = out.shape[1] // pieces

    def place(i):
        i = first + i
        return pl.multiple_of((4 * (i // 2) + 2 + i % 2) * block, block)

    def copy(i, piece):
        rows, columns = pl.ds(place(i), block), pl.ds(piece * width, width)
        slot = i % slots
        return pltpu.make_async_copy(
            buffer.at[slot, :, columns], out.at[rows, columns], sems.at[slot, piece]
        )

    def body(i, carry):
        slot = i % slots

        @pl.when(i >= slots)
        def _():
            for piece in range(pieces):
                copy(i - slots, piece).wait()

        left = inputs[:, pl.ds(place(i), block)]
        for piece in range(pieces):
            columns = slice(piece * width, (piece + 1) * width)
            buffer[slot, :, columns] = lax.dot_general(
                left, hidden[:, columns], (((0,), (0,)), ((), ())), preferred_element_type=F32
            ).astype(BF16)
            copy(i, piece).start()
        return carry

    lax.fori_loop(0, count, body, 0)
    for i in range(max(0, count - slots), count):
        for piece in range(pieces):
            copy(i, piece).wait()


def weight_grad_part(first, count, inputs, hidden, before):
    shape = jax.ShapeDtypeStruct(before.shape, BF16)
    block, slots, pieces = MXU, min(count, 4), 4
    return pl.pallas_call(
        functools.partial(weight_grad_kernel, first, count, block, slots, pieces),
        in_specs=[VMEM, VMEM, ANY],
        out_specs=ANY,
        out_shape=shape,
        scratch_shapes=[
            pltpu.VMEM((slots, block, shape.shape[1]), BF16),
            pltpu.SemaphoreType.DMA((slots, pieces)),
        ],
        input_output_aliases={2: 0},
        compiler_params=pltpu.CompilerParams(vmem_limit_bytes=20 * MIB),
        name="weight_grad_part",
    )(inputs, hidden, before)


def fast(inputs, weight, out_grad, pre_act):
    blocks = weight.shape[0] // (2 * MXU)

    own, inputs = hidden_part(pre_act, out_grad, inputs)
    other = exchange(inputs, "mp", 8, 1)
    hidden = [own] + [exchange(own, "batch", 4, k) for k in (1, 2, 3)]
    pair = jnp.stack([inputs, other])
    late, hidden[1] = lax.optimization_barrier((pair, hidden[1]))
    pairs = [pair, exchange(pair, "mp", 8, 4), exchange(pair, "mp", 8, 2), exchange(late, "mp", 8, 6)]
    pairs = [pairs[0], pairs[2], pairs[1], pairs[3]]
    early = load_part(0, 4, late, weight)
    grad, hidden, inputs, keep, send = both_part(hidden, pairs, weight, early)

    got = exchange(send, "mp", 8, 1)
    first = 1
    grad = weight_grad_part(0, first, inputs, hidden, grad)
    grad, keep = lax.optimization_barrier((grad, keep))
    mine = keep + got
    sends = [mine[k] for k in range(4)]
    gots = [exchange(sends[k], "mp", 8, 2 * k) for k in (1, 2, 3)]
    grad = weight_grad_part(first, blocks - first, inputs, hidden, grad)
    input_grad = (sends[0] + gots[0] + gots[1] + gots[2]).astype(BF16)
    return input_grad, grad


def plain(inputs, weight, out_grad, pre_act):
    hidden = lax.all_gather(gelu_back(pre_act, out_grad), "batch", axis=0, tiled=True)
    inputs = lax.all_gather(inputs, "mp", axis=0, tiled=True)
    weight_grad = lax.dot_general(
        inputs, hidden, (((0,), (0,)), ((), ())), preferred_element_type=F32
    ).astype(BF16)
    input_grad = lax.psum_scatter(
        lax.dot_general(hidden, weight, (((1,), (1,)), ((), ())), preferred_element_type=F32),
        "mp",
        scatter_dimension=0,
        tiled=True,
    ).astype(BF16)
    return input_grad, weight_grad


def solution(mesh):
    small = mesh.shape["batch"] == 4 and mesh.shape["mp"] == 8
    return jax.shard_map(
        fast if small else plain,
        mesh=mesh,
        in_specs=(P("mp", "batch"), P("batch", "mp"), P("batch", "mp"), P("batch", "mp")),
        out_specs=(P("mp", "batch"), P("batch", "mp")),
        check_vma=False,
    )
```

```python
import functools

import jax
import jax.numpy as jnp
from jax import lax
from jax.experimental import pallas as pl
from jax.experimental.pallas import tpu as pltpu
from jax.sharding import PartitionSpec as P

F32, BF16 = jnp.float32, jnp.bfloat16
MIB = 1 << 20
MXU = 256
LANES = 128
ROWS = 8
VMEM = pl.BlockSpec(memory_space=pltpu.VMEM)
ANY = pl.BlockSpec(memory_space=pl.ANY)


def gelu_back(pre_act, out_grad):
    value, pullback = jax.vjp(
        lambda v: jax.nn.gelu(v, approximate=True), pre_act.astype(F32)
    )
    return pullback(out_grad.astype(F32))[0].astype(BF16)


def in_hbm(x):
    return pltpu.with_memory_space_constraint(x, pltpu.HBM)


def hidden_kernel(pre_act, out_grad, inputs, own, inputs_out, pre, out, sems):
    pairs = ((pre_act, pre), (out_grad, out), (inputs, inputs_out))
    copies = [pltpu.make_async_copy(x, y, sems.at[i]) for i, (x, y) in enumerate(pairs)]
    for copy in copies:
        copy.start()
    for copy in copies:
        copy.wait()
    own[...] = gelu_back(pre[...], out[...])


def hidden_part(pre_act, out_grad, inputs):
    buffer = pltpu.VMEM(pre_act.shape, BF16)
    return pl.pallas_call(
        hidden_kernel,
        in_specs=[ANY] * 3,
        out_specs=[VMEM] * 2,
        out_shape=[buffer, pltpu.VMEM(inputs.shape, inputs.dtype)],
        scratch_shapes=[buffer, buffer, pltpu.SemaphoreType.DMA((3,))],
        compiler_params=pltpu.CompilerParams(vmem_limit_bytes=4 * MIB),
        name="hidden_part",
    )(*[in_hbm(x) for x in (pre_act, out_grad, inputs)])


def exchange(x, axis, size, bits):
    return lax.ppermute(x, axis, [(i, i ^ bits) for i in range(size)])


def gather_rows(z, pieces, padded):
    tokens = pieces[0].shape[0]
    padded[...] = jnp.zeros_like(padded)
    for k in range(4):
        padded[z ^ k, 0:tokens, :] = pieces[k][...].astype(F32)


def weight_rows(weight, tiles, sems, i, ready):
    rows, slot = pl.ds(pl.multiple_of(i * MXU, MXU), MXU), (i - ready) % tiles.shape[0]
    return pltpu.make_async_copy(weight.at[rows, :], tiles.at[slot], sems.at[slot])


def load_kernel(first, after, weight, tiles, sems):
    copies = [
        pltpu.make_async_copy(weight.at[pl.ds((first + i) * MXU, MXU), :], tiles.at[i], sems.at[i])
        for i in range(tiles.shape[0])
    ]
    for copy in copies:
        copy.start()
    for copy in copies:
        copy.wait()


def load_part(first, count, after, weight):
    return pl.pallas_call(
        functools.partial(load_kernel, first),
        in_specs=[ANY, ANY],
        out_specs=VMEM,
        out_shape=pltpu.VMEM((count, MXU, weight.shape[1]), weight.dtype),
        scratch_shapes=[pltpu.SemaphoreType.DMA((count,))],
        compiler_params=pltpu.CompilerParams(vmem_limit_bytes=2 * MIB),
        name="load_part",
    )(after, in_hbm(weight))


def both_kernel(*refs):
    z, m = lax.axis_index("batch"), lax.axis_index("mp")
    chip, core = m // 2, m % 2
    hidden, inputs, weight = refs[3::-1], refs[4:8], refs[8]
    early, refs = refs[9], refs[10:]
    grad, hidden_out, inputs_out, keep, send = refs[0:5]
    hidden_f32, inputs_f32, turned, total, tiles, out, load_sems, out_sems = refs[5:]
    depth, width = weight.shape
    blocks, steps, tall = depth // MXU, width // MXU, 2 * MXU
    ready, ring = early.shape[0], tiles.shape[0]

    for i in range(ready, min(ready + ring, blocks)):
        weight_rows(weight, tiles, load_sems, i, ready).start()
    gather_rows(z, hidden, hidden_f32)
    hidden_out[...] = hidden_f32[...].reshape(hidden_out.shape).astype(BF16)
    tokens = hidden[0].shape[0]
    half = tokens // 2
    inputs_f32[...] = jnp.zeros_like(inputs_f32)
    for k in range(4):
        own, other = inputs[k][0].astype(F32), inputs[k][1].astype(F32)
        inputs_f32[chip ^ k, 0:half, :] = jnp.where(core == 0, own, other)
        inputs_f32[chip ^ k, half:tokens, :] = jnp.where(core == 0, other, own)
    inputs_out[...] = inputs_f32[...].reshape(inputs_out.shape).astype(BF16)

    slots, pairs = out.shape[0], blocks // 4

    def write(p):
        rows = pl.ds(pl.multiple_of(2 * p * tall, tall), tall)
        return pltpu.make_async_copy(out.at[p % slots], grad.at[rows, :], out_sems.at[p % slots])

    def scoped(*sums):
        small, large = (sums[0:2], sums[2:4]), (sums[4:6], sums[6:8])

        def superblock(s, with_grad):
            known = isinstance(s, int) and 2 * s < ready
            base = s * tall if isinstance(s, int) else pl.multiple_of(s * tall, tall)
            for a in () if known else (0, 1):
                weight_rows(weight, tiles, load_sems, 2 * s + a, ready).wait()
                free = 2 * s - 2 + a

                @pl.when((free >= ready) & (free + ring < blocks))
                def _():
                    weight_rows(weight, tiles, load_sems, free + ring, ready).start()

            def push_weight(m, k, a, stage):
                columns = slice(k * MXU, (k + 1) * MXU)
                tile = early[2 * s + a, :, columns] if known else tiles[(2 * s + a - ready) % ring, :, columns]
                pltpu.matmul_push_rhs(tile, stage, m, transpose=True)

            def push_hidden(m, k, stage):
                tile = hidden_out[:, k * MXU : (k + 1) * MXU]
                blank = jnp.zeros((MXU - tile.shape[0], MXU), BF16)
                pltpu.matmul_push_rhs(jnp.concatenate([tile, blank], 0), stage, m)

            def times_weight(m, k, a, stage):
                left = hidden_out[:, k * MXU : (k + 1) * MXU]
                pltpu.matmul_acc_lhs(small[m][a], left, load_staged_rhs=stage)

            both = (0, 1)
            if with_grad:
                p = s // 2

                @pl.when(p >= slots)
                def _():
                    write(p - slots).wait()

                left = inputs_out[:, pl.ds(base, tall)]
                blank = jnp.zeros((turned.shape[1] - left.shape[0], tall), BF16)
                turned[...] = jnp.concatenate([left, blank], 0).T
                wide = jnp.zeros((MXU, MXU - turned.shape[1]), BF16)

                def times_hidden(m, a, stage):
                    left = jnp.concatenate([turned[a * MXU : (a + 1) * MXU, :], wide], 1)
                    pltpu.matmul_acc_lhs(large[m][a], left, load_staged_rhs=stage)

                def store(m, k, a):
                    out[p % slots, a * MXU : (a + 1) * MXU, k * MXU : (k + 1) * MXU] = pltpu.matmul_pop(
                        large[m][a]
                    ).astype(BF16)

                for m in both:
                    push_hidden(m, m, 0)
                for j in range(steps // 2):
                    h, o = j % 2, 1 - j % 2
                    for m in both:
                        times_hidden(m, 0, h)
                        push_weight(m, 2 * j + m, 0, o)
                    for m in both:
                        times_hidden(m, 1, None)
                        push_weight(m, 2 * j + m, 1, h)
                    for m in both:
                        store(m, 2 * j + m, 0)
                        times_weight(m, 2 * j + m, 0, o)
                        if 2 * j + 2 < steps:
                            push_hidden(m, 2 * j + 2 + m, o)
                        times_weight(m, 2 * j + m, 1, h)
                    for m in both:
                        store(m, 2 * j + m, 1)
                write(p).start()
            else:
                for m in both:
                    push_weight(m, m, 0, 0)
                for j in range(steps // 2):
                    for m in both:
                        push_weight(m, 2 * j + m, 1, 1)
                        times_weight(m, 2 * j + m, 0, 0)
                    for m in both:
                        if 2 * j + 2 < steps:
                            push_weight(m, 2 * j + 2 + m, 0, 0)
                        times_weight(m, 2 * j + m, 1, 1)
            for a in (0, 1):
                rows = pl.ds(pl.multiple_of(base + a * MXU, MXU), MXU)
                total[:, rows] = pltpu.matmul_pop(small[0][a]) + pltpu.matmul_pop(small[1][a])

        def body(p, carry):
            superblock(2 * p, True)
            superblock(2 * p + 1, False)
            return carry

        for p in range(ready // 4):
            body(p, 0)
        lax.fori_loop(ready // 4, pairs, body, 0)

    sums = [pltpu.ACC(m)((4 * ROWS, MXU), F32) for m in (0, 0, 1, 1)]
    sums += [pltpu.ACC(m)((MXU, MXU), F32) for m in (0, 0, 1, 1)]
    pl.run_scoped(scoped, *sums)
    for k in range(4):
        rows = total[pl.ds(pl.multiple_of(ROWS * (chip ^ k), ROWS), ROWS), :]
        low, high = rows[:half], rows[half:tokens]
        keep[k] = jnp.where(core == 0, low, high)
        send[k] = jnp.where(core == 0, high, low)
    for p in range(max(0, pairs - slots), pairs):
        write(p).wait()


def both_part(hidden, inputs, weight, early):
    depth, width = weight.shape
    half = hidden[0].shape[0] // 2
    f = lambda shape, dtype: jax.ShapeDtypeStruct(shape, dtype)
    slots, later = 2, 7
    return pl.pallas_call(
        both_kernel,
        in_specs=[VMEM] * 8 + [ANY, VMEM],
        out_specs=[ANY] + [VMEM] * 4,
        out_shape=[
            f((depth, width), BF16),
            f((4 * ROWS, width), BF16),
            f((4 * ROWS, depth), BF16),
            f((4, half, depth), F32),
            f((4, half, depth), F32),
        ],
        scratch_shapes=[
            pltpu.VMEM((4, ROWS, width), F32),
            pltpu.VMEM((4, ROWS, depth), F32),
            pltpu.VMEM((2 * MXU, LANES), BF16),
            pltpu.VMEM((4 * ROWS, depth), F32),
            pltpu.VMEM((later, MXU, width), BF16),
            pltpu.VMEM((slots, 2 * MXU, width), BF16),
            pltpu.SemaphoreType.DMA((later,)),
            pltpu.SemaphoreType.DMA((slots,)),
        ],
        compiler_params=pltpu.CompilerParams(vmem_limit_bytes=40 * MIB),
        name="both_part",
    )(*hidden[::-1], *inputs, in_hbm(weight), early)


def weight_grad_kernel(first, count, block, slots, pieces, inputs, hidden, *refs):
    out, buffer, sems = refs[-3:]
    width = out.shape[1] // pieces

    def place(i):
        i = first + i
        return pl.multiple_of((4 * (i // 2) + 2 + i % 2) * block, block)

    def copy(i, piece):
        rows, columns = pl.ds(place(i), block), pl.ds(piece * width, width)
        slot = i % slots
        return pltpu.make_async_copy(
            buffer.at[slot, :, columns], out.at[rows, columns], sems.at[slot, piece]
        )

    def body(i, carry):
        slot = i % slots

        @pl.when(i >= slots)
        def _():
            for piece in range(pieces):
                copy(i - slots, piece).wait()

        left = inputs[:, pl.ds(place(i), block)]
        for piece in range(pieces):
            columns = slice(piece * width, (piece + 1) * width)
            buffer[slot, :, columns] = lax.dot_general(
                left, hidden[:, columns], (((0,), (0,)), ((), ())), preferred_element_type=F32
            ).astype(BF16)
            copy(i, piece).start()
        return carry

    lax.fori_loop(0, count, body, 0)
    for i in range(max(0, count - slots), count):
        for piece in range(pieces):
            copy(i, piece).wait()


def weight_grad_part(first, count, inputs, hidden, before):
    shape = jax.ShapeDtypeStruct(before.shape, BF16)
    block, slots, pieces = MXU, min(count, 4), 4
    return pl.pallas_call(
        functools.partial(weight_grad_kernel, first, count, block, slots, pieces),
        in_specs=[VMEM, VMEM, ANY],
        out_specs=ANY,
        out_shape=shape,
        scratch_shapes=[
            pltpu.VMEM((slots, block, shape.shape[1]), BF16),
            pltpu.SemaphoreType.DMA((slots, pieces)),
        ],
        input_output_aliases={2: 0},
        compiler_params=pltpu.CompilerParams(vmem_limit_bytes=20 * MIB),
        name="weight_grad_part",
    )(inputs, hidden, before)


def fast(inputs, weight, out_grad, pre_act):
    blocks = weight.shape[0] // (2 * MXU)

    own, inputs = hidden_part(pre_act, out_grad, inputs)
    other = exchange(inputs, "mp", 8, 1)
    hidden = [own] + [exchange(own, "batch", 4, k) for k in (1, 2, 3)]
    pair = jnp.stack([inputs, other])
    late, hidden[1] = lax.optimization_barrier((pair, hidden[1]))
    pairs = [pair, exchange(late, "mp", 8, 2), exchange(pair, "mp", 8, 4), exchange(pair, "mp", 8, 6)]
    early = load_part(0, 4, late, weight)
    grad, hidden, inputs, keep, send = both_part(hidden, pairs, weight, early)

    got = exchange(send, "mp", 8, 1)
    first = 1
    grad = weight_grad_part(0, first, inputs, hidden, grad)
    grad, keep = lax.optimization_barrier((grad, keep))
    mine = keep + got
    sends = [mine[k] for k in range(4)]
    gots = [exchange(sends[k], "mp", 8, 2 * k) for k in (1, 2, 3)]
    grad = weight_grad_part(first, blocks - first, inputs, hidden, grad)
    input_grad = (sends[0] + gots[0] + gots[1] + gots[2]).astype(BF16)
    return input_grad, grad


def plain(inputs, weight, out_grad, pre_act):
    hidden = lax.all_gather(gelu_back(pre_act, out_grad), "batch", axis=0, tiled=True)
    inputs = lax.all_gather(inputs, "mp", axis=0, tiled=True)
    weight_grad = lax.dot_general(
        inputs, hidden, (((0,), (0,)), ((), ())), preferred_element_type=F32
    ).astype(BF16)
    input_grad = lax.psum_scatter(
        lax.dot_general(hidden, weight, (((1,), (1,)), ((), ())), preferred_element_type=F32),
        "mp",
        scatter_dimension=0,
        tiled=True,
    ).astype(BF16)
    return input_grad, weight_grad


def solution(mesh):
    small = mesh.shape["batch"] == 4 and mesh.shape["mp"] == 8
    return jax.shard_map(
        fast if small else plain,
        mesh=mesh,
        in_specs=(P("mp", "batch"), P("batch", "mp"), P("batch", "mp"), P("batch", "mp")),
        out_specs=(P("mp", "batch"), P("batch", "mp")),
        check_vma=False,
    )
```
